768 devices in a mesh: replica: 4 (over x), fsdp: 48 (over y, z_lo, core), tensor: 4 (over z_hi).
Axes of the slice: x: 4, y: 8, z: 12 (z_hi: 4, z_lo: 3; z = z_hi * 3 + z_lo), core: 2. Of those that a mesh axis runs over, the one named last changes fastest.
Arguments:
- tokens: bfloat16 [2, 49152, 5376], P(None, ('replica', 'fsdp', 'tensor')), may hold values from -24 to 24
- key_cot: bfloat16 [2, 49152, 512], P(None, ('replica', 'fsdp'), 'tensor'), may hold values from -6 to 6
- key_master: float32 [4, 5376, 512], P('replica', 'fsdp', 'tensor'), may hold values from -6 to 6
- adam_first: float32 [4, 5376, 512], P('replica', 'fsdp', 'tensor'), may hold values from -6 to 6
- adam_second: float32 [4, 5376, 512], P('replica', 'fsdp', 'tensor'), may hold values from 0.25 to 4
- frag_local: float32 [4, 8, 2, 5376, 512], P('replica', None, None, 'fsdp', 'tensor'), may hold values from -6 to 6
- frag_global: float32 [8, 2, 5376, 512], P(None, None, 'fsdp', 'tensor'), may hold values from -6 to 6
- frag_moment: float32 [8, 2, 5376, 512], P(None, None, 'fsdp', 'tensor'), may hold values from -3 to 3
- frag_order: int32 [8], replicated, may hold values from 0 to 7, each once
Outputs:
- keys: bfloat16 [2, 49152, 512], P(None, ('replica', 'fsdp'), 'tensor')
- new_master: float32 [4, 5376, 512], P('replica', 'fsdp', 'tensor')
- new_first: float32 [4, 5376, 512], P('replica', 'fsdp', 'tensor')
- new_second: float32 [4, 5376, 512], P('replica', 'fsdp', 'tensor')
- new_global: float32 [2, 5376, 512], P(None, 'fsdp', 'tensor')
- new_moment: float32 [2, 5376, 512], P(None, 'fsdp', 'tensor')
- mixed_local: float32 [4, 2, 5376, 512], P('replica', None, 'fsdp', 'tensor')
The draws below stay inside these ranges and needn't reach their ends.
Inputs may be any that keep to these rules, and one draw needn't show every extreme that they name: `frag_order`: each fragment appears once.
All inputs are finite; a program needn't handle non-finite values.
Results may differ from the reference program's by a relative error of at most 0.0049.
Values may be sent and summed in bfloat16 or wider, within the bound.
A program may use at most 64 MiB of HBM per device.

```python
import math
import jax
import jax.numpy as jnp
from jax import lax

D = 5376
C = 512
MICRO = 2
FRAGS = 8
FL = 2
TOKENS = 49152
N_REPLICA = 4


def strengthened(drawn, key, source, target, blocks, factor):
    def block_of(axis_at):
        return (jnp.arange(drawn.shape[axis_at]) // (drawn.shape[axis_at] // blocks)).reshape((-1,) + (1,) * (drawn.ndim - 1 - axis_at))

    first = jax.random.permutation(key, blocks)[block_of(target)]
    second = (block_of(target) + blocks // 2) % blocks
    return jnp.where((block_of(source) == first) | (block_of(source) == second), factor * drawn, drawn)


def shard_levels(rng, shape, cuts, low, top_value):
    factor_of = 1.0
    for axis_at, shards_of in cuts:
        heights = jax.random.uniform(jax.random.fold_in(jax.random.fold_in(rng, 6), axis_at), (shards_of,), jnp.float32, low / len(cuts), top_value / len(cuts))
        factor_of = factor_of * jnp.repeat(jnp.exp(heights), shape[axis_at] // shards_of).reshape((-1,) + (1,) * (len(shape) - 1 - axis_at))
    return factor_of


def scatter_about(own_key, shape, spread, bound, cuts=(), dtype=jnp.bfloat16):
    drawn = jax.random.normal(own_key, shape, jnp.float32) * spread
    if len(cuts) > 0:
        drawn = shard_levels(own_key, shape, cuts, -0.22, 0.18) * drawn
    return jnp.clip(drawn, min=-bound, max=bound).astype(dtype)


def gaussian_with(stream_key, dims, width, reach, pieces, heavy, kind=jnp.bfloat16):
    drawn = width * jax.random.normal(stream_key, dims, jnp.float32)
    if pieces:
        drawn = drawn * shard_levels(stream_key, dims, pieces, -0.22, 0.18)
    return jnp.clip(strengthened(drawn, jax.random.fold_in(stream_key, 3), *heavy), -reach, reach).astype(kind)


def setup_inputs(seed: int = 0) -> dict:
    splits = jax.random.split(jax.random.key(seed), 10)
    return {
        "tokens": gaussian_with(splits[0], (MICRO, TOKENS, D), 1.0, 24.0, ((1, 768),), (1, 2, 768, 6.0)),
        "key_cot": scatter_about(splits[1], (MICRO, TOKENS, C), 1.0, 6.0, ((1, 192), (2, 4))),
        "key_master": scatter_about(splits[2], (N_REPLICA, D, C), 1.0, 6.0, ((0, 4), (1, 48), (2, 4)), jnp.float32),
        "adam_first": scatter_about(splits[3], (N_REPLICA, D, C), 1.0, 6.0, ((0, 4), (1, 48), (2, 4)), jnp.float32),
        "adam_second": jnp.clip(jnp.exp(math.log(4.0) - 2.7725887 * jax.random.uniform(splits[4], (N_REPLICA, D, C), jnp.float32) ** shard_levels(splits[4], (N_REPLICA, D, C), ((0, 4), (1, 48), (2, 4)), -0.2, 0.2)), 0.25, 4.0),
        "frag_local": scatter_about(splits[5], (N_REPLICA, FRAGS, FL, D, C), 1.0, 6.0, ((0, 4), (3, 48), (4, 4)), jnp.float32),
        "frag_global": scatter_about(splits[6], (FRAGS, FL, D, C), 1.0, 6.0, ((2, 48), (3, 4)), jnp.float32),
        "frag_moment": scatter_about(splits[7], (FRAGS, FL, D, C), 0.5, 3.0, ((2, 48), (3, 4)), jnp.float32),
        "frag_order": jax.random.permutation(splits[8], FRAGS).astype(jnp.int32),
    }


def reference(tokens, key_cot, key_master, adam_first, adam_second, frag_local, frag_global, frag_moment, frag_order):
    factor = D ** (-0.5)
    weights_bf = key_master.astype(jnp.bfloat16)
    span = TOKENS // N_REPLICA
    key_blocks = []
    grad_blocks = []
    for replica in range(N_REPLICA):
        token_rows = tokens[:, replica * span:(replica + 1) * span].reshape(MICRO * span, D)
        cot_rows = key_cot[:, replica * span:(replica + 1) * span].reshape(MICRO * span, C)
        projected = factor * jnp.dot(token_rows, weights_bf[replica], preferred_element_type=jnp.float32)
        key_blocks.append(projected.astype(jnp.bfloat16).reshape(MICRO, span, C))
        summed = lax.dot_general(token_rows, cot_rows, (((0,), (0,)), ((), ())), preferred_element_type=jnp.float32)
        grad_blocks.append(factor * summed)
    keys = jnp.concatenate(key_blocks, 1)
    gradient = jnp.stack(grad_blocks)
    new_first = 0.9 * adam_first + 0.1 * gradient
    new_second = 0.95 * adam_second + 0.05 * gradient * gradient
    first_hat = new_first / (1.0 - 0.9 ** 10)
    second_hat = new_second / (1.0 - 0.95 ** 10)
    new_master = key_master - 0.01 * (first_hat / (jnp.sqrt(second_hat) + 1e-08) + 0.1 * key_master)
    chosen = frag_order[0]
    local_frag = lax.dynamic_index_in_dim(frag_local, chosen, 1, keepdims=False)
    global_frag = lax.dynamic_index_in_dim(frag_global, chosen, 0, keepdims=False)
    moment_frag = lax.dynamic_index_in_dim(frag_moment, chosen, 0, keepdims=False)
    drift = global_frag[None] - local_frag
    outer_grad = lax.optimization_barrier(jnp.sum(drift, 0)) / N_REPLICA
    new_moment = 0.9 * moment_frag + outer_grad
    new_global = global_frag - 0.7 * (outer_grad + 0.9 * new_moment)
    mixed_local = 0.5 * local_frag + 0.5 * new_global[None]
    return (keys, new_master, new_first, new_second, new_global, new_moment, mixed_local)
```

```python
import jax
import jax.numpy as jnp
from jax import lax
from jax.experimental import pallas as pl
from jax.experimental.pallas import tpu as pltpu
from jax.sharding import PartitionSpec as P

D = 5376
NX, NY, NZ = 4, 8, 12
LO = 3
ROWS = D // 48
BLOCK = D // NY
PAIR = 2 * ROWS
HALF = D // 2
WIDE = 256
MESH = pl.DeviceIdType.MESH
BF, F32 = jnp.bfloat16, jnp.float32


def place(x, y, z, core):
    return (x, (y * LO + z % LO) * 2 + core, z // LO)


def exchange(
    tok, cot, master, order, local,
    keys, landed, frags,
    tokbuf, cotbuf, cotwide, own_w, wbuf, gbuf, first, ring, zsend, kbuf, localbuf,
    local_sem, tok_sem, cot_send, cot_recv, wy_send, wy_recv, wz_send, wz_recv,
    first_send, ring_send, ring_recv, gz_send, gz_recv, key_send, key_recv, fr_send, fr_recv,
):
    x = lax.axis_index("replica")
    fsdp = lax.axis_index("fsdp")
    z_hi = lax.axis_index("tensor")
    core = fsdp % 2
    y = fsdp // (2 * LO)
    z_lo = (fsdp // 2) % LO
    z = z_hi * LO + z_lo
    half = z_hi // 2
    side = z_hi % 2
    other = 1 - core
    pending = []

    def remote(src, dst, send, recv, target):
        return pltpu.make_async_remote_copy(
            src_ref=src, dst_ref=dst, send_sem=send, recv_sem=recv, device_id=target, device_id_type=MESH
        )

    def arrived(dst, send, recv):
        remote(dst, dst, send, recv, place(x, y, z, other)).wait_recv()

    barrier = pltpu.get_barrier_semaphore()
    friends = [place(x, y, z, other)]
    friends += [place(x, (y + j) % NY, z, c) for j in range(1, NY) for c in range(2)]
    friends += [place(x, y, (z + j) % NZ, c) for j in range(1, NZ) for c in range(2)]
    friends += [place((x + j) % NX, y, z, core) for j in range(1, NX)]
    for friend in friends:
        pl.semaphore_signal(barrier, inc=1, device_id=friend, device_id_type=MESH)

    tok_rows = tokbuf.at[pl.ds(pl.multiple_of(core * 128, 128), 128)]
    tok_local = pltpu.make_async_copy(tok, tok_rows, local_sem.at[0])
    tok_local.start()
    frag_local = pltpu.make_async_copy(local, localbuf, local_sem.at[1])
    frag_local.start()
    own_w[...] = master[0].astype(BF)

    pl.semaphore_wait(barrier, len(friends))

    for zt in range(4):
        target_z = zt * LO + z_lo
        src = cot.at[:, pl.ds(zt * 64, 64), :]
        dst = cotbuf.at[side, core]
        here = (z_hi == zt) & (core == half)
        copy = remote(src, dst, cot_send.at[zt], cot_recv.at[side * 2 + core], place(x, y, target_z, half))

        @pl.when(here)
        def _(src=src, dst=dst):
            dst[...] = src[...]

        @pl.when(jnp.logical_not(here))
        def _(copy=copy):
            copy.start()

        pending.append((jnp.logical_not(here), copy))

    tok_copy = remote(tok, tok_rows, tok_sem.at[0], tok_sem.at[1], place(x, y, z, other))
    tok_copy.start()
    pending.append((None, tok_copy))

    lanes = pl.ds(pl.multiple_of(side * 128, 128), 128)
    w_rows = pl.ds(pl.multiple_of(z_lo * PAIR + core * ROWS, 16), ROWS)
    for j in range(1, NY):
        copy = remote(
            own_w, wbuf.at[y, w_rows, lanes], wy_send.at[j], wy_recv.at[y * 2 + core],
            place(x, (y + j) % NY, z, half),
        )
        copy.start()
        pending.append((None, copy))
    stays = core == half
    leaves = core != half

    @pl.when(stays)
    def _():
        wbuf[y, w_rows, lanes] = own_w[...]

    copy = remote(own_w, wbuf.at[y, w_rows, lanes], wy_send.at[0], wy_recv.at[y * 2 + core], place(x, y, z, other))

    @pl.when(leaves)
    def _(copy=copy):
        copy.start()

    pending.append((leaves, copy))

    frag_local.wait()
    frags[x] = localbuf[order[0]]
    for j in range(1, NX):
        copy = remote(
            frags.at[x], frags.at[x], fr_send.at[j], fr_recv.at[x], place((x + j) % NX, y, z, core)
        )
        copy.start()
        pending.append((None, copy))

    def unit(source, part):
        return wbuf.at[
            pl.ds(part * 4, 4),
            pl.ds(pl.multiple_of((source % LO) * PAIR, 16), PAIR),
            pl.ds(pl.multiple_of(((source // LO) % 2) * 128, 128), 128),
        ]

    def reach(direction, part):
        return 6 if direction == part else 5

    def w_send(source, direction, part, step, when):
        target = place(x, y, (z + (1, NZ - 1)[direction]) % NZ, core)
        copy = remote(
            unit(source, part), unit(source, part),
            wz_send.at[direction * 2 + part, step], wz_recv.at[direction * 2 + part, step], target,
        )

        @pl.when(when)
        def _():
            copy.start()

        pending.append((when, copy))

    def w_step(step):
        for direction in range(2):
            for part in range(2):
                if step > reach(direction, part):
                    continue
                source = (z + (NZ - step, step)[direction]) % NZ
                mine = source // 6 == core

                @pl.when(mine)
                def _(source=source, direction=direction, part=part):
                    arrived(
                        unit(source, part),
                        wz_send.at[direction * 2 + part, step],
                        wz_recv.at[direction * 2 + part, step],
                    )

                if step < reach(direction, part):
                    w_send(source, direction, part, step + 1, mine)

    for part in range(2):
        for from_y in range(part * 4, part * 4 + 4):
            for c in range(2):

                @pl.when(stays & ((y != from_y) | (core != c)))
                def _(from_y=from_y, c=c):
                    arrived(
                        wbuf.at[from_y, pl.ds(pl.multiple_of(z_lo * PAIR + c * ROWS, 16), ROWS), lanes],
                        wy_send.at[0],
                        wy_recv.at[from_y * 2 + c],
                    )

        for direction in range(2):
            w_send(z, direction, part, 1, stays)

    for t in range(2):
        for c in range(2):
            source_hi = core * 2 + t

            @pl.when((source_hi != z_hi) | (core != c))
            def _(t=t, c=c):
                arrived(cotbuf.at[t, c], cot_send.at[0], cot_recv.at[t * 2 + c])

    for t in range(2):
        cotwide[:, pl.ds(t * 128, 128)] = cotbuf[t].reshape(256, 128)
    tok_local.wait()
    arrived(tokbuf.at[pl.ds(pl.multiple_of(other * 128, 128), 128)], tok_sem.at[0], tok_sem.at[1])

    def tile(i, carry):
        columns = pl.ds(pl.multiple_of(i * WIDE, WIDE), WIDE)
        gbuf[columns, :] = lax.dot_general(
            tokbuf[:, columns], cotwide[...], (((0,), (0,)), ((), ())), preferred_element_type=F32
        )
        return carry

    lax.fori_loop(0, D // WIDE, tile, 0)

    def part_of(at_y, sub):
        return gbuf[pl.ds(pl.multiple_of(at_y * BLOCK, 8), BLOCK), pl.ds(sub * 128, 128)]

    def hops(direction, sub):
        return 4 if direction == sub else 3

    def g_send(src, direction, sub, step, send):
        lane = direction * 2 + sub
        copy = remote(
            src, ring.at[lane, step - 1], send, ring_recv.at[lane, step],
            place(x, (y + (1, NY - 1)[direction]) % NY, z, core),
        )
        copy.start()
        pending.append((None, copy))

    for sub in range(2):
        for direction in range(2):
            far = hops(direction, sub)
            lane = direction * 2 + sub
            first[lane] = part_of((y + (far, NY - far)[direction]) % NY, sub).astype(BF)
            g_send(first.at[lane], direction, sub, 1, first_send.at[lane])

    def g_step(step, sub):
        for direction in range(2):
            far = hops(direction, sub)
            lane = direction * 2 + sub
            if step > far:
                continue
            arrived(ring.at[lane, step - 1], ring_send.at[lane, step], ring_recv.at[lane, step])
            if step < far:
                left = far - step
                block = part_of((y + (left, NY - left)[direction]) % NY, sub)
                ring[lane, step - 1] = (ring[lane, step - 1].astype(F32) + block).astype(BF)
                g_send(ring.at[lane, step - 1], direction, sub, step + 1, ring_send.at[lane, step])

    def g_end(sub):
        total = part_of(y, sub)
        for direction in range(2):
            total = total + ring[direction * 2 + sub, hops(direction, sub) - 1].astype(F32)
        zsend[sub] = total.astype(BF)
        for lo in range(LO):
            for c in range(2):
                target_z = (core * 2 + sub) * LO + lo
                rows = pl.ds((lo * 2 + c) * ROWS, ROWS)
                here = (target_z == z) & (core == c)
                copy = remote(
                    zsend.at[sub, rows], landed.at[z], gz_send.at[sub * 6 + lo * 2 + c], gz_recv.at[z],
                    place(x, y, target_z, c),
                )

                @pl.when(here)
                def _(rows=rows):
                    landed[z] = zsend[sub, rows]

                @pl.when(jnp.logical_not(here))
                def _(copy=copy):
                    copy.start()

                pending.append((jnp.logical_not(here), copy))

    w_step(1)
    g_step(1, 0)
    w_step(2)
    g_step(1, 1)
    w_step(3)
    g_step(2, 0)
    g_step(2, 1)
    w_step(4)
    g_step(3, 0)
    w_step(5)
    g_step(3, 1)
    g_step(4, 0)
    g_end(0)
    g_step(4, 1)
    g_end(1)
    w_step(6)

    total = jnp.dot(tokbuf[:, pl.ds(0, HALF)], wbuf[pl.ds(0, 4)].reshape(HALF, 256), preferred_element_type=F32)
    total = total + jnp.dot(
        tokbuf[:, pl.ds(HALF, HALF)], wbuf[pl.ds(4, 4)].reshape(HALF, 256), preferred_element_type=F32
    )
    total = (D ** (-0.5) * total).astype(BF)
    for t in range(2):
        kbuf[t] = total[:, t * 128 : t * 128 + 128].reshape(2, 2, 64, 128)
    spot = keys.at[:, pl.ds(pl.multiple_of(z_hi * 64, 64), 64), :]
    for t in range(2):
        for c in range(2):
            target_hi = core * 2 + t
            here = (target_hi == z_hi) & (core == c)
            copy = remote(
                kbuf.at[t, c], spot, key_send.at[t * 2 + c], key_recv.at[z_hi],
                place(x, y, target_hi * LO + z_lo, c),
            )

            @pl.when(here)
            def _(t=t, c=c):
                spot[...] = kbuf[t, c]

            @pl.when(jnp.logical_not(here))
            def _(copy=copy):
                copy.start()

            pending.append((jnp.logical_not(here), copy))

    for j in range(1, NX):
        from_x = (x + j) % NX
        arrived(frags.at[from_x], fr_send.at[0], fr_recv.at[from_x])
    for from_z in range(NZ):

        @pl.when((z != from_z) | leaves)
        def _(from_z=from_z):
            arrived(landed.at[from_z], gz_send.at[0], gz_recv.at[from_z])

    for hi in range(4):

        @pl.when((z_hi != hi) | leaves)
        def _(hi=hi):
            arrived(keys.at[:, pl.ds(hi * 64, 64), :], key_send.at[0], key_recv.at[hi])

    for when, copy in pending:
        if when is None:
            copy.wait_send()
        else:

            @pl.when(when)
            def _(copy=copy):
                copy.wait_send()


def update(
    order, keys_in, landed, frags, master, first, second, frag_global, frag_moment,
    keys, new_master, new_first, new_second, new_global, new_moment, mixed,
):
    keys[...] = keys_in[...]
    gradient = landed[0].astype(F32)
    for from_z in range(1, NZ):
        gradient = gradient + landed[from_z].astype(F32)
    gradient = D ** (-0.5) * gradient
    weights = master[0]
    one = 0.9 * first[0] + 0.1 * gradient
    two = 0.95 * second[0] + 0.05 * gradient * gradient
    one_hat = one / (1.0 - 0.9**10)
    two_hat = two / (1.0 - 0.95**10)
    new_master[0] = weights - 0.01 * (one_hat / (jnp.sqrt(two_hat) + 1e-08) + 0.1 * weights)
    new_first[0] = one
    new_second[0] = two
    chosen = order[0]
    held = frag_global[chosen]
    drift = held - frags[0]
    for replica in range(1, NX):
        drift = drift + (held - frags[replica])
    share = drift / NX
    moment = 0.9 * frag_moment[chosen] + share
    after = held - 0.7 * (share + 0.9 * moment)
    new_moment[...] = moment
    new_global[...] = after
    mixed[0] = 0.5 * frags[lax.axis_index("replica")] + 0.5 * after


def on_device(
    tokens, key_cot, key_master, adam_first, adam_second, frag_local, frag_global, frag_moment, frag_order
):
    vmem = pl.BlockSpec(memory_space=pltpu.VMEM)
    smem = pl.BlockSpec(memory_space=pltpu.SMEM)
    anywhere = pl.BlockSpec(memory_space=pl.ANY)
    shape = jax.ShapeDtypeStruct
    dma = pltpu.SemaphoreType.DMA
    keys, landed, frags = pl.pallas_call(
        exchange,
        out_shape=(
            shape((2, 256, 128), BF),
            shape((NZ, ROWS, 128), BF),
            shape((NX, 2, ROWS, 128), F32),
        ),
        in_specs=[anywhere, vmem, vmem, smem, anywhere],
        out_specs=(vmem, vmem, vmem),
        scratch_shapes=[
            pltpu.VMEM((256, D), BF),
            pltpu.VMEM((2, 2, 2, 64, 128), BF),
            pltpu.VMEM((256, 256), BF),
            pltpu.VMEM((ROWS, 128), BF),
            pltpu.VMEM((NY, BLOCK, 256), BF),
            pltpu.VMEM((D, 256), F32),
            pltpu.VMEM((4, BLOCK, 128), BF),
            pltpu.VMEM((4, 4, BLOCK, 128), BF),
            pltpu.VMEM((2, BLOCK, 128), BF),
            pltpu.VMEM((2, 2, 2, 64, 128), BF),
            pltpu.VMEM(frag_local.shape[1:], F32),
            dma((2,)), dma((2,)), dma((4,)), dma((4,)), dma((NY,)), dma((2 * NY,)), dma((4, 7)), dma((4, 7)),
            dma((4,)), dma((4, 5)), dma((4, 5)), dma((12,)), dma((NZ,)), dma((4,)), dma((4,)), dma((NX,)), dma((NX,)),
        ],
        compiler_params=pltpu.CompilerParams(
            collective_id=0, has_side_effects=True, vmem_limit_bytes=48 * 1024 * 1024
        ),
    )(tokens.reshape(128, D), key_cot, key_master, frag_order, frag_local[0])
    return pl.pallas_call(
        update,
        out_shape=(
            shape((2, 256, 128), BF),
            shape((1, ROWS, 128), F32),
            shape((1, ROWS, 128), F32),
            shape((1, ROWS, 128), F32),
            shape((2, ROWS, 128), F32),
            shape((2, ROWS, 128), F32),
            shape((1, 2, ROWS, 128), F32),
        ),
        in_specs=[smem] + [vmem] * 8,
        out_specs=(vmem,) * 7,
        compiler_params=pltpu.CompilerParams(vmem_limit_bytes=32 * 1024 * 1024),
    )(frag_order, keys, landed, frags, key_master, adam_first, adam_second, frag_global, frag_moment)


def solution(mesh):
    return jax.shard_map(
        on_device,
        mesh=mesh,
        in_specs=(
            P(None, ("replica", "fsdp", "tensor"), None),
            P(None, ("replica", "fsdp"), "tensor"),
            P("replica", "fsdp", "tensor"),
            P("replica", "fsdp", "tensor"),
            P("replica", "fsdp", "tensor"),
            P("replica", None, None, "fsdp", "tensor"),
            P(None, None, "fsdp", "tensor"),
            P(None, None, "fsdp", "tensor"),
            P(),
        ),
        out_specs=(
            P(None, ("replica", "fsdp"), "tensor"),
            P("replica", "fsdp", "tensor"),
            P("replica", "fsdp", "tensor"),
            P("replica", "fsdp", "tensor"),
            P(None, "fsdp", "tensor"),
            P(None, "fsdp", "tensor"),
            P("replica", None, "fsdp", "tensor"),
        ),
        check_vma=False,
    )
```

```python
import jax
import jax.numpy as jnp
from jax import lax
from jax.experimental import pallas as pl
from jax.experimental.pallas import tpu as pltpu
from jax.sharding import PartitionSpec as P

D = 5376
NX, NY, NZ = 4, 8, 12
LO = 3
ROWS = D // 48
BLOCK = D // NY
PAIR = 2 * ROWS
HALF = D // 2
SHORT = BLOCK // 2
WIDE = 256
TILES = D // WIDE
PARTS = 4
SPAN = NY // PARTS
EARLY = 9
MESH = pl.DeviceIdType.MESH
BF, F32 = jnp.bfloat16, jnp.float32


def place(x, y, z, core):
    return (x, (y * LO + z % LO) * 2 + core, z // LO)


def exchange(
    tok, cot, master_in, first_in, second_in, order_in, local_in, global_in, moment_in,
    keys, new_master, new_first, new_second, new_global, new_moment, mixed,
    tokbuf, cotbuf, cotwide, own_w, wbuf, gbuf, lead_out, ring, zsend, kbuf, landed, frags,
    order, local, held, momentum, master, first, second, adam_out, outer_out,
    local_sem, tok_sem, cot_send, cot_recv, wy_send, wy_recv, wz_send, wz_recv,
    first_send, ring_send, ring_recv, gz_send, gz_recv, key_send, key_recv, fr_send, fr_recv,
):
    x = lax.axis_index("replica")
    fsdp = lax.axis_index("fsdp")
    z_hi = lax.axis_index("tensor")
    core = fsdp % 2
    y = fsdp // (2 * LO)
    z_lo = (fsdp // 2) % LO
    z = z_hi * LO + z_lo
    other = 1 - core
    in_charge = core == 1
    helps = core == 0
    pending = []

    def remote(src, dst, send, recv, target):
        return pltpu.make_async_remote_copy(
            src_ref=src, dst_ref=dst, send_sem=send, recv_sem=recv, device_id=target, device_id_type=MESH
        )

    def arrived(dst, send, recv):
        remote(dst, dst, send, recv, place(x, y, z, other)).wait_recv()

    loads = []
    for i, (src, dst) in enumerate((
        (master_in.at[0], master), (order_in, order), (local_in, local), (first_in.at[0], first),
        (second_in.at[0], second), (global_in, held), (moment_in, momentum),
    )):
        loads.append(pltpu.make_async_copy(src, dst, local_sem.at[i + 1]))
    tok_rows = tokbuf.at[pl.ds(pl.multiple_of(core * 128, 128), 128)]
    tok_local = pltpu.make_async_copy(tok, tok_rows, local_sem.at[0])
    for copy in (loads[0], loads[1], tok_local, loads[2]):
        copy.start()

    barrier = pltpu.get_barrier_semaphore()
    friends = [place(x, y, z, other)]
    friends += [place(x, (y + j) % NY, z, c) for j in range(1, NY) for c in range(2)]
    friends += [place(x, y, (z + j) % NZ, c) for j in range(1, NZ) for c in range(2)]
    friends += [place((x + j) % NX, y, z, core) for j in range(1, NX)]
    for friend in friends:
        pl.semaphore_signal(barrier, inc=1, device_id=friend, device_id_type=MESH)

    loads[0].wait()
    own_w[...] = master[...].astype(BF)

    pl.semaphore_wait(barrier, len(friends))

    for zt in range(4):
        src = cot.at[:, pl.ds(zt * 64, 64), :]
        dst = cotbuf.at[z_hi, core]
        here = (z_hi == zt) & helps
        copy = remote(src, dst, cot_send.at[zt], cot_recv.at[z_hi * 2 + core], place(x, y, zt * LO + z_lo, 0))
        mine = pltpu.make_async_copy(src, dst, local_sem.at[8])

        @pl.when(here)
        def _(mine=mine):
            mine.start()
            mine.wait()

        @pl.when(jnp.logical_not(here))
        def _(copy=copy):
            copy.start()

        pending.append((jnp.logical_not(here), copy))

    tok_copy = remote(tok, tok_rows, tok_sem.at[0], tok_sem.at[1], place(x, y, z, other))
    tok_copy.start()
    pending.append((None, tok_copy))

    w_rows = pl.ds(pl.multiple_of(z_lo * PAIR + core * ROWS, 16), ROWS)
    w_spot = wbuf.at[z_hi, y, w_rows]
    for j in range(1, NY):
        copy = remote(own_w, w_spot, wy_send.at[j], wy_recv.at[y * 2 + core], place(x, (y + j) % NY, z, 1))
        copy.start()
        pending.append((None, copy))

    @pl.when(in_charge)
    def _():
        wbuf[z_hi, y, w_rows] = own_w[...]

    copy = remote(own_w, w_spot, wy_send.at[0], wy_recv.at[y * 2 + core], place(x, y, z, other))

    @pl.when(helps)
    def _(copy=copy):
        copy.start()

    pending.append((helps, copy))

    loads[1].wait()
    loads[2].wait()
    frags[x] = local[order[0]]
    for j in range(1, NX):
        copy = remote(
            frags.at[x], frags.at[x], fr_send.at[j], fr_recv.at[x], place((x + j) % NX, y, z, core)
        )
        copy.start()
        pending.append((None, copy))

    for copy in loads[3:]:
        copy.start()

    def tokens_here():
        tok_local.wait()
        arrived(tokbuf.at[pl.ds(pl.multiple_of(other * 128, 128), 128)], tok_sem.at[0], tok_sem.at[1])

    outer_stores = [
        pltpu.make_async_copy(outer_out.at[i], dst, local_sem.at[9 + i])
        for i, dst in enumerate((new_global, new_moment, mixed.at[0]))
    ]

    def outer_step():
        for j in range(1, NX):
            from_x = (x + j) % NX
            arrived(frags.at[from_x], fr_send.at[0], fr_recv.at[from_x])
        loads[5].wait()
        loads[6].wait()
        before = held[order[0]]
        drift = before - frags[0]
        for replica in range(1, NX):
            drift = drift + (before - frags[replica])
        share = drift / NX
        moment = 0.9 * momentum[order[0]] + share
        after = before - 0.7 * (share + 0.9 * moment)
        outer_out[0] = after
        outer_out[1] = moment
        outer_out[2] = 0.5 * frags[x] + 0.5 * after
        for copy in outer_stores:
            copy.start()

    def make_keys():
        sent = []

        def unit(source, part):
            rows = pl.ds(pl.multiple_of(source % LO * PAIR, 16), PAIR)
            return wbuf.at[source // LO, pl.ds(part * SPAN, SPAN), rows]

        def reach(direction, part):
            return 6 if part % 2 == direction else 5

        def send(source, direction, part, step):
            lane = direction * PARTS + part
            copy = remote(
                unit(source, part), unit(source, part), wz_send.at[lane, step], wz_recv.at[lane, step],
                place(x, y, (z + (1, NZ - 1)[direction]) % NZ, 1),
            )
            copy.start()
            sent.append(copy)

        def own(part):
            for from_y in range(part * SPAN, part * SPAN + SPAN):
                for c in range(2):

                    @pl.when((y != from_y) | (core != c))
                    def _(from_y=from_y, c=c):
                        rows = pl.ds(pl.multiple_of(z_lo * PAIR + c * ROWS, 16), ROWS)
                        arrived(wbuf.at[z_hi, from_y, rows], wy_send.at[0], wy_recv.at[from_y * 2 + c])

            for direction in range(2):
                send(z, direction, part, 1)

        def forward(step, part):
            for direction in range(2):
                if step > reach(direction, part):
                    continue
                source = (z + (NZ - step, step)[direction]) % NZ
                lane = direction * PARTS + part
                arrived(unit(source, part), wz_send.at[lane, step], wz_recv.at[lane, step])
                if step < reach(direction, part):
                    send(source, direction, part, step + 1)

        def keys_of(ahead):
            head = (z_hi + ahead) % 4
            total = jnp.zeros((256, 128), F32)
            for part in range(2):
                total = total + jnp.dot(
                    tokbuf[:, pl.ds(part * HALF, HALF)],
                    wbuf[head, pl.ds(part * 4, 4)].reshape(HALF, 128),
                    preferred_element_type=F32,
                )
            kbuf[ahead] = (D ** (-0.5) * total).astype(BF).reshape(2, 2, 64, 128)
            spot = keys.at[:, pl.ds(pl.multiple_of(z_hi * 64, 64), 64), :]
            for c in range(2):
                if ahead == 0 and c == 1:
                    copy = pltpu.make_async_copy(kbuf.at[ahead, c], spot, local_sem.at[8])
                    copy.start()
                    copy.wait()
                    continue
                copy = remote(
                    kbuf.at[ahead, c], spot, key_send.at[ahead * 2 + c], key_recv.at[z_hi],
                    place(x, y, head * LO + z_lo, c),
                )
                copy.start()
                sent.append(copy)

        own(0)
        sent.pop(0).wait_send()
        sent.pop(0).wait_send()
        own(1)
        line, begun, done, near, wide = [(0, 0), (0, 1)], 2, 0, False, False
        while done < len(line):
            step, part = line[done][0] + 1, line[done][1]
            done += 1
            forward(step, part)
            if step < 6:
                line.append((step, part))
            if begun < PARTS:
                own(begun)
                line.append((0, begun))
                begun += 1
            if done == 2 * PARTS:
                outer_step()
            rest = [at for at, _ in line[done:]]
            if not near and begun == PARTS and all(at >= 2 for at in rest):
                near = True
                tokens_here()
                keys_of(0)
            if not wide and near and all(at >= 5 for at in rest):
                wide = True
                keys_of(1)
                keys_of(3)
        keys_of(2)
        for copy in sent:
            copy.wait_send()

    def make_gradient():
        sent = []
        for t in range(4):
            for c in range(2):

                @pl.when((t != z_hi) | (core != c))
                def _(t=t, c=c):
                    arrived(cotbuf.at[t, c], cot_send.at[0], cot_recv.at[t * 2 + c])

        for t in range(4):
            cotwide[:, pl.ds(t * 128, 128)] = cotbuf[t].reshape(256, 128)
        tokens_here()
        lead = (((y + 3) % NY) * BLOCK) // WIDE

        def tile(i, carry):
            columns = pl.ds(pl.multiple_of(((lead + i) % TILES) * WIDE, WIDE), WIDE)
            gbuf[columns, :] = lax.dot_general(
                tokbuf[:, columns], cotwide[...], (((0,), (0,)), ((), ())), preferred_element_type=F32
            )
            return carry

        def part_of(at_y, sub):
            rows = pl.ds(pl.multiple_of(at_y * BLOCK + sub % 2 * SHORT, 8), SHORT)
            return gbuf[rows, pl.ds(sub // 2 * 256, 256)]

        def hops(direction, sub):
            return 4 if direction == sub // 2 else 3

        def send(src, direction, sub, step, sem):
            lane = direction * 4 + sub
            copy = remote(
                src, ring.at[lane, step - 1], sem, ring_recv.at[lane, step],
                place(x, (y + (1, NY - 1)[direction]) % NY, z, 0),
            )
            copy.start()
            sent.append(copy)

        def members(group):
            return [(sub, direction) for sub in (group, group + 2) for direction in range(2)]

        def begin(group):
            for sub, direction in members(group):
                far = hops(direction, sub)
                lane = direction * 4 + sub
                lead_out[lane] = part_of((y + (far, NY - far)[direction]) % NY, sub).astype(BF)
                send(lead_out.at[lane], direction, sub, 1, first_send.at[lane])

        def pass_on(step, group):
            for sub, direction in members(group):
                far = hops(direction, sub)
                lane = direction * 4 + sub
                if step > far:
                    continue
                arrived(ring.at[lane, step - 1], ring_send.at[lane, step], ring_recv.at[lane, step])
                if step < far:
                    left = far - step
                    block = part_of((y + (left, NY - left)[direction]) % NY, sub)
                    ring[lane, step - 1] = (ring[lane, step - 1].astype(F32) + block).astype(BF)
                    send(ring.at[lane, step - 1], direction, sub, step + 1, ring_send.at[lane, step])

        def finish(group):
            for sub in (group, group + 2):
                total = part_of(y, sub)
                for direction in range(2):
                    total = total + ring[direction * 4 + sub, hops(direction, sub) - 1].astype(F32)
                for k in range(2):
                    zsend[sub, k] = total[:, k * 128 : k * 128 + 128].astype(BF)
                    for i in range(3):
                        lo, c = divmod(group * 3 + i, 2)
                        target_z = (sub // 2 * 2 + k) * LO + lo
                        piece = zsend.at[sub, k, pl.ds(i * ROWS, ROWS)]
                        copy = remote(
                            piece, landed.at[z], gz_send.at[(sub * 2 + k) * 3 + i], gz_recv.at[z],
                            place(x, y, target_z, c),
                        )
                        if c == 1:
                            copy.start()
                            sent.append(copy)
                            continue
                        away = target_z != z

                        @pl.when(jnp.logical_not(away))
                        def _(sub=sub, k=k, i=i):
                            landed[z] = zsend[sub, k, pl.ds(i * ROWS, ROWS)]

                        @pl.when(away)
                        def _(copy=copy):
                            copy.start()

                        maybe.append((away, copy))

        maybe = []
        lax.fori_loop(0, EARLY, tile, 0)
        begin(0)
        lax.fori_loop(EARLY, TILES, tile, 0)
        begin(1)
        pass_on(1, 0)
        pass_on(1, 1)
        outer_step()
        for step in (2, 3):
            for group in range(2):
                pass_on(step, group)
        pass_on(4, 0)
        finish(0)
        pass_on(4, 1)
        finish(1)
        for copy in sent:
            copy.wait_send()
        for when, copy in maybe:

            @pl.when(when)
            def _(copy=copy):
                copy.wait_send()

    @pl.when(in_charge)
    def _():
        make_keys()

    @pl.when(helps)
    def _():
        make_gradient()

    for from_z in range(NZ):

        @pl.when((z != from_z) | in_charge)
        def _(from_z=from_z):
            arrived(landed.at[from_z], gz_send.at[0], gz_recv.at[from_z])

    loads[3].wait()
    loads[4].wait()
    gradient = landed[0].astype(F32)
    for from_z in range(1, NZ):
        gradient = gradient + landed[from_z].astype(F32)
    gradient = D ** (-0.5) * gradient
    weights = master[...]
    one = 0.9 * first[...] + 0.1 * gradient
    two = 0.95 * second[...] + 0.05 * gradient * gradient
    one_hat = one / (1.0 - 0.9**10)
    two_hat = two / (1.0 - 0.95**10)
    adam_out[0] = weights - 0.01 * (one_hat / (jnp.sqrt(two_hat) + 1e-08) + 0.1 * weights)
    adam_out[1] = one
    adam_out[2] = two
    stores = outer_stores
    for i, dst in enumerate((new_master, new_first, new_second)):
        stores.append(pltpu.make_async_copy(adam_out.at[i], dst.at[0], local_sem.at[12 + i]))
        stores[-1].start()

    for hi in range(4):

        @pl.when((z_hi != hi) | helps)
        def _(hi=hi):
            arrived(keys.at[:, pl.ds(hi * 64, 64), :], key_send.at[0], key_recv.at[hi])

    for copy in stores:
        copy.wait()
    for when, copy in pending:
        if when is None:
            copy.wait_send()
        else:

            @pl.when(when)
            def _(copy=copy):
                copy.wait_send()


def hand_over(*refs):
    count = (len(refs) - 1) // 3
    sources, results, buffers, sems = refs[:count], refs[count : 2 * count], refs[2 * count : -1], refs[-1]
    inward = [
        pltpu.make_async_copy(src, buf, sems.at[i]) for i, (src, buf) in enumerate(zip(sources, buffers))
    ]
    outward = [
        pltpu.make_async_copy(buf, dst, sems.at[count + i])
        for i, (buf, dst) in enumerate(zip(buffers, results))
    ]
    for copy in inward:
        copy.start()
    for first, second in zip(inward, outward):
        first.wait()
        second.start()
    for copy in outward:
        copy.wait()


def on_device(
    tokens, key_cot, key_master, adam_first, adam_second, frag_local, frag_global, frag_moment, frag_order
):
    hbm = pl.BlockSpec(memory_space=pltpu.HBM)
    shape = jax.ShapeDtypeStruct
    dma = pltpu.SemaphoreType.DMA
    one = (ROWS, 128)
    two = (2, *one)
    results = (shape((2, 256, 128), BF),) + (shape((1, *one), F32),) * 3 + (shape(two, F32),) * 2 + (shape((1, *two), F32),)
    made = pl.pallas_call(
        exchange,
        out_shape=results,
        in_specs=[hbm] * 9,
        out_specs=(hbm,) * 7,
        scratch_shapes=[
            pltpu.VMEM((256, D), BF),
            pltpu.VMEM((4, 2, 2, 64, 128), BF),
            pltpu.VMEM((256, 512), BF),
            pltpu.VMEM(one, BF),
            pltpu.VMEM((4, NY, BLOCK, 128), BF),
            pltpu.VMEM((D, 512), F32),
            pltpu.VMEM((8, SHORT, 256), BF),
            pltpu.VMEM((8, 4, SHORT, 256), BF),
            pltpu.VMEM((4, 2, SHORT, 128), BF),
            pltpu.VMEM((4, 2, 2, 64, 128), BF),
            pltpu.VMEM((NZ, *one), BF),
            pltpu.VMEM((NX, *two), F32),
            pltpu.SMEM((8,), jnp.int32),
            pltpu.VMEM((8, *two), F32),
            pltpu.VMEM((8, *two), F32),
            pltpu.VMEM((8, *two), F32),
            pltpu.VMEM(one, F32),
            pltpu.VMEM(one, F32),
            pltpu.VMEM(one, F32),
            pltpu.VMEM((3, *one), F32),
            pltpu.VMEM((3, *two), F32),
            dma((15,)), dma((2,)), dma((4,)), dma((8,)), dma((NY,)), dma((2 * NY,)), dma((2 * PARTS, 7)), dma((2 * PARTS, 7)),
            dma((8,)), dma((8, 5)), dma((8, 5)), dma((24,)), dma((NZ,)), dma((8,)), dma((4,)), dma((NX,)), dma((NX,)),
        ],
        compiler_params=pltpu.CompilerParams(
            collective_id=0, has_side_effects=True, vmem_limit_bytes=60 * 1024 * 1024
        ),
    )(
        tokens.reshape(128, D), key_cot, key_master, adam_first, adam_second, frag_order, frag_local[0],
        frag_global, frag_moment,
    )
    return pl.pallas_call(
        hand_over,
        out_shape=results,
        in_specs=[hbm] * 7,
        out_specs=(hbm,) * 7,
        scratch_shapes=[pltpu.VMEM(r.shape, r.dtype) for r in results] + [dma((14,))],
        compiler_params=pltpu.CompilerParams(vmem_limit_bytes=60 * 1024 * 1024),
    )(*made)


def solution(mesh):
    return jax.shard_map(
        on_device,
        mesh=mesh,
        in_specs=(
            P(None, ("replica", "fsdp", "tensor"), None),
            P(None, ("replica", "fsdp"), "tensor"),
            P("replica", "fsdp", "tensor"),
            P("replica", "fsdp", "tensor"),
            P("replica", "fsdp", "tensor"),
            P("replica", None, None, "fsdp", "tensor"),
            P(None, None, "fsdp", "tensor"),
            P(None, None, "fsdp", "tensor"),
            P(),
        ),
        out_specs=(
            P(None, ("replica", "fsdp"), "tensor"),
            P("replica", "fsdp", "tensor"),
            P("replica", "fsdp", "tensor"),
            P("replica", "fsdp", "tensor"),
            P(None, "fsdp", "tensor"),
            P(None, "fsdp", "tensor"),
            P("replica", None, "fsdp", "tensor"),
        ),
        check_vma=False,
    )
```

```python
import jax
import jax.numpy as jnp
from jax import lax
from jax.experimental import pallas as pl
from jax.experimental.pallas import tpu as pltpu
from jax.sharding import PartitionSpec as P

D = 5376
NX, NY, NZ = 4, 8, 12
LO = 3
ROWS = D // 48
BLOCK = D // NY
PAIR = 2 * ROWS
HALF = D // 2
SHORT = BLOCK // 2
WIDE = 256
TILES = D // WIDE
PARTS = 4
SPAN = NY // PARTS
MESH = pl.DeviceIdType.MESH
BF, F32 = jnp.bfloat16, jnp.float32


def place(x, y, z, core):
    return (x, (y * LO + z % LO) * 2 + core, z // LO)


def exchange(
    tok, cot, master_in, first_in, second_in, order_in, local_in, global_in, moment_in,
    keys, new_master, new_first, new_second, new_global, new_moment, mixed,
    tokbuf, cotbuf, cotwide, own_w, wbuf, gbuf, lead_out, ring, zsend, kbuf, landed, frags,
    order, local, held, momentum, master, first, second, adam_out, outer_out,
    local_sem, tok_sem, cot_send, cot_recv, wy_send, wy_recv, wz_send, wz_recv,
    first_send, ring_send, ring_recv, gz_send, gz_recv, key_send, key_recv, fr_send, fr_recv,
):
    x = lax.axis_index("replica")
    fsdp = lax.axis_index("fsdp")
    z_hi = lax.axis_index("tensor")
    core = fsdp % 2
    y = fsdp // (2 * LO)
    z_lo = (fsdp // 2) % LO
    z = z_hi * LO + z_lo
    other = 1 - core
    in_charge = core == 1
    helps = core == 0
    pending = []

    def remote(src, dst, send, recv, target):
        return pltpu.make_async_remote_copy(
            src_ref=src, dst_ref=dst, send_sem=send, recv_sem=recv, device_id=target, device_id_type=MESH
        )

    def arrived(dst, send, recv):
        remote(dst, dst, send, recv, place(x, y, z, other)).wait_recv()

    loads = []
    for i, (src, dst) in enumerate((
        (master_in.at[0], master), (order_in, order), (local_in, local), (first_in.at[0], first),
        (second_in.at[0], second), (global_in, held), (moment_in, momentum),
    )):
        loads.append(pltpu.make_async_copy(src, dst, local_sem.at[i + 1]))
    tok_rows = tokbuf.at[pl.ds(pl.multiple_of(core * 128, 128), 128)]
    tok_local = pltpu.make_async_copy(tok, tok_rows, local_sem.at[0])
    for copy in (loads[0], loads[1], tok_local, loads[2]):
        copy.start()

    barrier = pltpu.get_barrier_semaphore()
    friends = [place(x, y, z, other)]
    friends += [place(x, (y + j) % NY, z, c) for j in range(1, NY) for c in range(2)]
    friends += [place(x, y, (z + j) % NZ, c) for j in range(1, NZ) for c in range(2)]
    friends += [place((x + j) % NX, y, z, core) for j in range(1, NX)]
    for friend in friends:
        pl.semaphore_signal(barrier, inc=1, device_id=friend, device_id_type=MESH)

    loads[0].wait()
    own_w[...] = master[...].astype(BF)

    pl.semaphore_wait(barrier, len(friends))

    for zt in range(4):
        src = cot.at[:, pl.ds(zt * 64, 64), :]
        dst = cotbuf.at[z_hi, core]
        here = (z_hi == zt) & helps
        copy = remote(src, dst, cot_send.at[zt], cot_recv.at[z_hi * 2 + core], place(x, y, zt * LO + z_lo, 0))
        mine = pltpu.make_async_copy(src, dst, local_sem.at[8])

        @pl.when(here)
        def _(mine=mine):
            mine.start()
            mine.wait()

        @pl.when(jnp.logical_not(here))
        def _(copy=copy):
            copy.start()

        pending.append((jnp.logical_not(here), copy))

    tok_copy = remote(tok, tok_rows, tok_sem.at[0], tok_sem.at[1], place(x, y, z, other))
    tok_copy.start()
    pending.append((None, tok_copy))

    w_rows = pl.ds(pl.multiple_of(z_lo * PAIR + core * ROWS, 16), ROWS)
    w_spot = wbuf.at[z_hi, y, w_rows]
    for j in (1, 7, 2, 6, 3, 5, 4):
        copy = remote(own_w, w_spot, wy_send.at[j], wy_recv.at[y * 2 + core], place(x, (y + j) % NY, z, 1))
        copy.start()
        pending.append((None, copy))

    @pl.when(in_charge)
    def _():
        wbuf[z_hi, y, w_rows] = own_w[...]

    copy = remote(own_w, w_spot, wy_send.at[0], wy_recv.at[y * 2 + core], place(x, y, z, other))

    @pl.when(helps)
    def _(copy=copy):
        copy.start()

    pending.append((helps, copy))

    loads[1].wait()
    loads[2].wait()
    frags[x] = local[order[0]]
    for j in range(1, NX):
        copy = remote(
            frags.at[x], frags.at[x], fr_send.at[j], fr_recv.at[x], place((x + j) % NX, y, z, core)
        )
        copy.start()
        pending.append((None, copy))

    for copy in loads[3:]:
        copy.start()

    def tokens_here():
        tok_local.wait()
        arrived(tokbuf.at[pl.ds(pl.multiple_of(other * 128, 128), 128)], tok_sem.at[0], tok_sem.at[1])

    outer_stores = [
        pltpu.make_async_copy(outer_out.at[i], dst, local_sem.at[9 + i])
        for i, dst in enumerate((new_global, new_moment, mixed.at[0]))
    ]

    def outer_step():
        for j in range(1, NX):
            from_x = (x + j) % NX
            arrived(frags.at[from_x], fr_send.at[0], fr_recv.at[from_x])
        loads[5].wait()
        loads[6].wait()
        before = held[order[0]]
        drift = before - frags[0]
        for replica in range(1, NX):
            drift = drift + (before - frags[replica])
        share = drift / NX
        moment = 0.9 * momentum[order[0]] + share
        after = before - 0.7 * (share + 0.9 * moment)
        outer_out[0] = after
        outer_out[1] = moment
        outer_out[2] = 0.5 * frags[x] + 0.5 * after
        for copy in outer_stores:
            copy.start()

    def make_keys():
        sent = []

        def first_y(part):
            return (y // SPAN * SPAN + (0, 2, 6, 4)[part]) % NY

        def unit(source, part):
            rows = pl.ds(pl.multiple_of(source % LO * PAIR, 16), PAIR)
            return wbuf.at[source // LO, pl.ds(first_y(part), SPAN), rows]

        def reach(direction, part):
            return 6 if part % 2 == direction else 5

        def send(source, direction, part, step):
            lane = direction * PARTS + part
            copy = remote(
                unit(source, part), unit(source, part), wz_send.at[lane, step], wz_recv.at[lane, step],
                place(x, y, (z + (1, NZ - 1)[direction]) % NZ, 1),
            )
            copy.start()
            sent.append(copy)

        def own(part):
            for i in range(SPAN):
                from_y = first_y(part) + i
                for c in range(2):

                    @pl.when((y != from_y) | (core != c))
                    def _(from_y=from_y, c=c):
                        rows = pl.ds(pl.multiple_of(z_lo * PAIR + c * ROWS, 16), ROWS)
                        arrived(wbuf.at[z_hi, from_y, rows], wy_send.at[0], wy_recv.at[from_y * 2 + c])

            for direction in range(2):
                send(z, direction, part, 1)

        def forward(step, part):
            for direction in range(2):
                if step > reach(direction, part):
                    continue
                source = (z + (NZ - step, step)[direction]) % NZ
                lane = direction * PARTS + part
                arrived(unit(source, part), wz_send.at[lane, step], wz_recv.at[lane, step])
                if step < reach(direction, part):
                    send(source, direction, part, step + 1)

        def keys_of(ahead):
            head = (z_hi + ahead) % 4
            total = jnp.zeros((256, 128), F32)
            for part in range(2):
                total = total + jnp.dot(
                    tokbuf[:, pl.ds(part * HALF, HALF)],
                    wbuf[head, pl.ds(part * 4, 4)].reshape(HALF, 128),
                    preferred_element_type=F32,
                )
            kbuf[ahead] = (D ** (-0.5) * total).astype(BF).reshape(2, 2, 64, 128)
            spot = keys.at[:, pl.ds(pl.multiple_of(z_hi * 64, 64), 64), :]
            for c in range(2):
                if ahead == 0 and c == 1:
                    copy = pltpu.make_async_copy(kbuf.at[ahead, c], spot, local_sem.at[8])
                    copy.start()
                    copy.wait()
                    continue
                copy = remote(
                    kbuf.at[ahead, c], spot, key_send.at[ahead * 2 + c], key_recv.at[z_hi],
                    place(x, y, head * LO + z_lo, c),
                )
                copy.start()
                sent.append(copy)

        own(0)
        sent.pop(0).wait_send()
        sent.pop(0).wait_send()
        own(1)
        line, begun, done, near, wide = [(0, 0), (0, 1)], 2, 0, False, False
        while done < len(line):
            step, part = line[done][0] + 1, line[done][1]
            done += 1
            forward(step, part)
            if step < 6:
                line.append((step, part))
            if begun < PARTS:
                own(begun)
                line.append((0, begun))
                begun += 1
            if done == 2 * PARTS:
                outer_step()
            rest = [at for at, _ in line[done:]]
            if not near and begun == PARTS and all(at >= 2 for at in rest):
                near = True
                tokens_here()
                keys_of(0)
            if not wide and near and all(at >= 5 for at in rest):
                wide = True
                keys_of(1)
                keys_of(3)
        keys_of(2)
        for copy in sent:
            copy.wait_send()

    def make_gradient():
        sent = []
        for t in range(4):
            for c in range(2):

                @pl.when((t != z_hi) | (core != c))
                def _(t=t, c=c):
                    arrived(cotbuf.at[t, c], cot_send.at[0], cot_recv.at[t * 2 + c])

        for t in range(4):
            cotwide[:, pl.ds(t * 128, 128)] = cotbuf[t].reshape(256, 128)
        tokens_here()

        far_tile = (((y + 4) % NY) * BLOCK) // WIDE
        near_tile = (((y + 3) % NY) * BLOCK) // WIDE

        def tile(i, lead):
            columns = pl.ds(pl.multiple_of(((lead + i) % TILES) * WIDE, WIDE), WIDE)
            gbuf[columns, :] = lax.dot_general(
                tokbuf[:, columns], cotwide[...], (((0,), (0,)), ((), ())), preferred_element_type=F32
            )
            return lead

        def part_of(at_y, sub):
            rows = pl.ds(pl.multiple_of(at_y * BLOCK + sub % 2 * SHORT, 8), SHORT)
            return gbuf[rows, pl.ds(sub // 2 * 256, 256)]

        def hops(direction, sub):
            return 4 if direction == sub // 2 else 3

        def send(src, direction, sub, step, sem):
            lane = direction * 4 + sub
            copy = remote(
                src, ring.at[lane, step - 1], sem, ring_recv.at[lane, step],
                place(x, (y + (1, NY - 1)[direction]) % NY, z, 0),
            )
            copy.start()
            sent.append(copy)

        def begin(sub):
            for direction in range(2):
                far = hops(direction, sub)
                lane = direction * 4 + sub
                lead_out[lane] = part_of((y + (far, NY - far)[direction]) % NY, sub).astype(BF)
                send(lead_out.at[lane], direction, sub, 1, first_send.at[lane])

        def pass_on(step, sub):
            for direction in range(2):
                far = hops(direction, sub)
                lane = direction * 4 + sub
                if step > far:
                    continue
                arrived(ring.at[lane, step - 1], ring_send.at[lane, step], ring_recv.at[lane, step])
                if step < far:
                    left = far - step
                    block = part_of((y + (left, NY - left)[direction]) % NY, sub)
                    ring[lane, step - 1] = (ring[lane, step - 1].astype(F32) + block).astype(BF)
                    send(ring.at[lane, step - 1], direction, sub, step + 1, ring_send.at[lane, step])

        def finish(sub):
            total = part_of(y, sub)
            for direction in range(2):
                total = total + ring[direction * 4 + sub, hops(direction, sub) - 1].astype(F32)
            for k in range(2):
                zsend[sub, k] = total[:, k * 128 : k * 128 + 128].astype(BF)
                for i in range(3):
                    lo, c = divmod(sub % 2 * 3 + i, 2)
                    target_z = (sub // 2 * 2 + k) * LO + lo
                    piece = zsend.at[sub, k, pl.ds(i * ROWS, ROWS)]
                    copy = remote(
                        piece, landed.at[z], gz_send.at[(sub * 2 + k) * 3 + i], gz_recv.at[z],
                        place(x, y, target_z, c),
                    )
                    if c == 1:
                        copy.start()
                        sent.append(copy)
                        continue
                    away = target_z != z

                    @pl.when(jnp.logical_not(away))
                    def _(k=k, i=i):
                        landed[z] = zsend[sub, k, pl.ds(i * ROWS, ROWS)]

                    @pl.when(away)
                    def _(copy=copy):
                        copy.start()

                    maybe.append((away, copy))

        maybe = []
        lax.fori_loop(0, 7, tile, far_tile)
        begin(0)
        lax.fori_loop(0, 3, tile, near_tile)
        begin(2)
        lax.fori_loop(7, 11, tile, far_tile)
        begin(1)
        lax.fori_loop(11, 15, tile, far_tile)
        begin(3)
        lax.fori_loop(15, 19, tile, far_tile)
        for step in range(1, 5):
            for sub in (0, 2, 1, 3):
                pass_on(step, sub)
                if step == 4:
                    finish(sub)
            if step == 1:
                outer_step()
        for copy in sent:
            copy.wait_send()
        for when, copy in maybe:

            @pl.when(when)
            def _(copy=copy):
                copy.wait_send()

    @pl.when(in_charge)
    def _():
        make_keys()

    @pl.when(helps)
    def _():
        make_gradient()

    for from_z in range(NZ):

        @pl.when((z != from_z) | in_charge)
        def _(from_z=from_z):
            arrived(landed.at[from_z], gz_send.at[0], gz_recv.at[from_z])

    loads[3].wait()
    loads[4].wait()
    gradient = landed[0].astype(F32)
    for from_z in range(1, NZ):
        gradient = gradient + landed[from_z].astype(F32)
    gradient = D ** (-0.5) * gradient
    weights = master[...]
    one = 0.9 * first[...] + 0.1 * gradient
    two = 0.95 * second[...] + 0.05 * gradient * gradient
    one_hat = one / (1.0 - 0.9**10)
    two_hat = two / (1.0 - 0.95**10)
    adam_out[0] = weights - 0.01 * (one_hat / (jnp.sqrt(two_hat) + 1e-08) + 0.1 * weights)
    adam_out[1] = one
    adam_out[2] = two
    stores = outer_stores
    for i, dst in enumerate((new_master, new_first, new_second)):
        stores.append(pltpu.make_async_copy(adam_out.at[i], dst.at[0], local_sem.at[12 + i]))
        stores[-1].start()

    for hi in range(4):

        @pl.when((z_hi != hi) | helps)
        def _(hi=hi):
            arrived(keys.at[:, pl.ds(hi * 64, 64), :], key_send.at[0], key_recv.at[hi])

    for copy in stores:
        copy.wait()
    for when, copy in pending:
        if when is None:
            copy.wait_send()
        else:

            @pl.when(when)
            def _(copy=copy):
                copy.wait_send()


def hand_over(*refs):
    count = (len(refs) - 1) // 3
    sources, results, buffers, sems = refs[:count], refs[count : 2 * count], refs[2 * count : -1], refs[-1]
    inward = [
        pltpu.make_async_copy(src, buf, sems.at[i]) for i, (src, buf) in enumerate(zip(sources, buffers))
    ]
    outward = [
        pltpu.make_async_copy(buf, dst, sems.at[count + i])
        for i, (buf, dst) in enumerate(zip(buffers, results))
    ]
    for copy in inward:
        copy.start()
    for first, second in zip(inward, outward):
        first.wait()
        second.start()
    for copy in outward:
        copy.wait()


def on_device(
    tokens, key_cot, key_master, adam_first, adam_second, frag_local, frag_global, frag_moment, frag_order
):
    hbm = pl.BlockSpec(memory_space=pltpu.HBM)
    shape = jax.ShapeDtypeStruct
    dma = pltpu.SemaphoreType.DMA
    one = (ROWS, 128)
    two = (2, *one)
    results = (shape((2, 256, 128), BF),) + (shape((1, *one), F32),) * 3 + (shape(two, F32),) * 2 + (shape((1, *two), F32),)
    made = pl.pallas_call(
        exchange,
        out_shape=results,
        in_specs=[hbm] * 9,
        out_specs=(hbm,) * 7,
        scratch_shapes=[
            pltpu.VMEM((256, D), BF),
            pltpu.VMEM((4, 2, 2, 64, 128), BF),
            pltpu.VMEM((256, 512), BF),
            pltpu.VMEM(one, BF),
            pltpu.VMEM((4, NY, BLOCK, 128), BF),
            pltpu.VMEM((D, 512), F32),
            pltpu.VMEM((8, SHORT, 256), BF),
            pltpu.VMEM((8, 4, SHORT, 256), BF),
            pltpu.VMEM((4, 2, SHORT, 128), BF),
            pltpu.VMEM((4, 2, 2, 64, 128), BF),
            pltpu.VMEM((NZ, *one), BF),
            pltpu.VMEM((NX, *two), F32),
            pltpu.SMEM((8,), jnp.int32),
            pltpu.VMEM((8, *two), F32),
            pltpu.VMEM((8, *two), F32),
            pltpu.VMEM((8, *two), F32),
            pltpu.VMEM(one, F32),
            pltpu.VMEM(one, F32),
            pltpu.VMEM(one, F32),
            pltpu.VMEM((3, *one), F32),
            pltpu.VMEM((3, *two), F32),
            dma((15,)), dma((2,)), dma((4,)), dma((8,)), dma((NY,)), dma((2 * NY,)), dma((2 * PARTS, 7)), dma((2 * PARTS, 7)),
            dma((8,)), dma((8, 5)), dma((8, 5)), dma((24,)), dma((NZ,)), dma((8,)), dma((4,)), dma((NX,)), dma((NX,)),
        ],
        compiler_params=pltpu.CompilerParams(
            collective_id=0, has_side_effects=True, vmem_limit_bytes=60 * 1024 * 1024
        ),
    )(
        tokens.reshape(128, D), key_cot, key_master, adam_first, adam_second, frag_order, frag_local[0],
        frag_global, frag_moment,
    )
    return pl.pallas_call(
        hand_over,
        out_shape=results,
        in_specs=[hbm] * 7,
        out_specs=(hbm,) * 7,
        scratch_shapes=[pltpu.VMEM(r.shape, r.dtype) for r in results] + [dma((14,))],
        compiler_params=pltpu.CompilerParams(vmem_limit_bytes=60 * 1024 * 1024),
    )(*made)


def solution(mesh):
    return jax.shard_map(
        on_device,
        mesh=mesh,
        in_specs=(
            P(None, ("replica", "fsdp", "tensor"), None),
            P(None, ("replica", "fsdp"), "tensor"),
            P("replica", "fsdp", "tensor"),
            P("replica", "fsdp", "tensor"),
            P("replica", "fsdp", "tensor"),
            P("replica", None, None, "fsdp", "tensor"),
            P(None, None, "fsdp", "tensor"),
            P(None, None, "fsdp", "tensor"),
            P(),
        ),
        out_specs=(
            P(None, ("replica", "fsdp"), "tensor"),
            P("replica", "fsdp", "tensor"),
            P("replica", "fsdp", "tensor"),
            P("replica", "fsdp", "tensor"),
            P(None, "fsdp", "tensor"),
            P(None, "fsdp", "tensor"),
            P("replica", None, "fsdp", "tensor"),
        ),
        check_vma=False,
    )
```

```python
import jax
import jax.numpy as jnp
from jax import lax
from jax.experimental import pallas as pl
from jax.experimental.pallas import tpu as pltpu
from jax.sharding import PartitionSpec as P

D = 5376
NX, NY, NZ = 4, 8, 12
LO = 3
ROWS = D // 48
BLOCK = D // NY
PAIR = 2 * ROWS
HALF = D // 2
SHORT = BLOCK // 2
WIDE = 256
TILES = D // WIDE
PARTS = 4
SPAN = NY // PARTS
MESH = pl.DeviceIdType.MESH
BF, F32 = jnp.bfloat16, jnp.float32


def place(x, y, z, core):
    return (x, (y * LO + z % LO) * 2 + core, z // LO)


def exchange(
    tok, cot, master_in, first_in, second_in, order_in, local_in, global_in, moment_in,
    keys, new_master, new_first, new_second, new_global, new_moment, mixed,
    tokbuf, cotbuf, cotwide, own_w, wbuf, gbuf, lead_out, ring, zsend, kbuf, landed, frags,
    order, local, held, momentum, master, first, second, adam_out, outer_out,
    local_sem, tok_sem, cot_send, cot_recv, wy_send, wy_recv, wz_send, wz_recv,
    first_send, ring_send, ring_recv, gz_send, gz_recv, key_send, key_recv, fr_send, fr_recv,
):
    x = lax.axis_index("replica")
    fsdp = lax.axis_index("fsdp")
    z_hi = lax.axis_index("tensor")
    core = fsdp % 2
    y = fsdp // (2 * LO)
    z_lo = (fsdp // 2) % LO
    z = z_hi * LO + z_lo
    other = 1 - core
    in_charge = core == 1
    helps = core == 0
    pending = []

    def remote(src, dst, send, recv, target):
        return pltpu.make_async_remote_copy(
            src_ref=src, dst_ref=dst, send_sem=send, recv_sem=recv, device_id=target, device_id_type=MESH
        )

    def arrived(dst, send, recv):
        remote(dst, dst, send, recv, place(x, y, z, other)).wait_recv()

    loads = []
    for i, (src, dst) in enumerate((
        (master_in.at[0], master), (order_in, order), (local_in, local), (first_in.at[0], first),
        (second_in.at[0], second), (global_in, held), (moment_in, momentum),
    )):
        loads.append(pltpu.make_async_copy(src, dst, local_sem.at[i + 1]))
    tok_rows = tokbuf.at[pl.ds(pl.multiple_of(core * 128, 128), 128)]
    tok_local = pltpu.make_async_copy(tok, tok_rows, local_sem.at[0])
    for copy in (loads[0], loads[1], tok_local, loads[2]):
        copy.start()

    barrier = pltpu.get_barrier_semaphore()
    friends = [place(x, y, z, other)]
    friends += [place(x, (y + j) % NY, z, c) for j in range(1, NY) for c in range(2)]
    friends += [place(x, y, (z + j) % NZ, c) for j in range(1, NZ) for c in range(2)]
    friends += [place((x + j) % NX, y, z, core) for j in range(1, NX)]
    for friend in friends:
        pl.semaphore_signal(barrier, inc=1, device_id=friend, device_id_type=MESH)

    loads[0].wait()
    own_w[...] = master[...].astype(BF)

    pl.semaphore_wait(barrier, len(friends))

    for zt in range(4):
        src = cot.at[:, pl.ds(zt * 64, 64), :]
        dst = cotbuf.at[z_hi, core]
        here = (z_hi == zt) & helps
        copy = remote(src, dst, cot_send.at[zt], cot_recv.at[z_hi * 2 + core], place(x, y, zt * LO + z_lo, 0))
        mine = pltpu.make_async_copy(src, dst, local_sem.at[8])

        @pl.when(here)
        def _(mine=mine):
            mine.start()
            mine.wait()

        @pl.when(jnp.logical_not(here))
        def _(copy=copy):
            copy.start()

        pending.append((jnp.logical_not(here), copy))

    tok_copy = remote(tok, tok_rows, tok_sem.at[0], tok_sem.at[1], place(x, y, z, other))
    tok_copy.start()
    pending.append((None, tok_copy))

    w_rows = pl.ds(pl.multiple_of(z_lo * PAIR + core * ROWS, 16), ROWS)
    w_spot = wbuf.at[z_hi, y, w_rows]
    for j in (1, 7, 2, 6, 3, 5, 4):
        copy = remote(own_w, w_spot, wy_send.at[j], wy_recv.at[y * 2 + core], place(x, (y + j) % NY, z, 1))
        copy.start()
        pending.append((None, copy))

    @pl.when(in_charge)
    def _():
        wbuf[z_hi, y, w_rows] = own_w[...]

    copy = remote(own_w, w_spot, wy_send.at[0], wy_recv.at[y * 2 + core], place(x, y, z, other))

    @pl.when(helps)
    def _(copy=copy):
        copy.start()

    pending.append((helps, copy))

    loads[1].wait()
    loads[2].wait()
    frags[x] = local[order[0]]
    for j in range(1, NX):
        copy = remote(
            frags.at[x], frags.at[x], fr_send.at[j], fr_recv.at[x], place((x + j) % NX, y, z, core)
        )
        copy.start()
        pending.append((None, copy))

    for copy in loads[3:]:
        copy.start()

    def tokens_here():
        tok_local.wait()
        arrived(tokbuf.at[pl.ds(pl.multiple_of(other * 128, 128), 128)], tok_sem.at[0], tok_sem.at[1])

    outer_stores = [
        pltpu.make_async_copy(outer_out.at[i], dst, local_sem.at[9 + i])
        for i, dst in enumerate((new_global, new_moment, mixed.at[0]))
    ]

    def outer_step():
        for j in range(1, NX):
            from_x = (x + j) % NX
            arrived(frags.at[from_x], fr_send.at[0], fr_recv.at[from_x])
        loads[5].wait()
        loads[6].wait()
        before = held[order[0]]
        drift = before - frags[0]
        for replica in range(1, NX):
            drift = drift + (before - frags[replica])
        share = drift / NX
        moment = 0.9 * momentum[order[0]] + share
        after = before - 0.7 * (share + 0.9 * moment)
        outer_out[0] = after
        outer_out[1] = moment
        outer_out[2] = 0.5 * frags[x] + 0.5 * after
        for copy in outer_stores:
            copy.start()

    def make_keys():
        sent = []

        def first_y(part):
            return (y // SPAN * SPAN + (0, 2, 6, 4)[part]) % NY

        def unit(source, part):
            rows = pl.ds(pl.multiple_of(source % LO * PAIR, 16), PAIR)
            return wbuf.at[source // LO, pl.ds(first_y(part), SPAN), rows]

        def reach(direction, part):
            return 6 if part % 2 == direction else 5

        def send(source, direction, part, step):
            lane = direction * PARTS + part
            copy = remote(
                unit(source, part), unit(source, part), wz_send.at[lane, step], wz_recv.at[lane, step],
                place(x, y, (z + (1, NZ - 1)[direction]) % NZ, 1),
            )
            copy.start()
            sent.append(copy)

        def own(part):
            for i in range(SPAN):
                from_y = first_y(part) + i
                for c in range(2):

                    @pl.when((y != from_y) | (core != c))
                    def _(from_y=from_y, c=c):
                        rows = pl.ds(pl.multiple_of(z_lo * PAIR + c * ROWS, 16), ROWS)
                        arrived(wbuf.at[z_hi, from_y, rows], wy_send.at[0], wy_recv.at[from_y * 2 + c])

            for direction in range(2):
                send(z, direction, part, 1)

        def forward(step, part):
            for direction in range(2):
                if step > reach(direction, part):
                    continue
                source = (z + (NZ - step, step)[direction]) % NZ
                lane = direction * PARTS + part
                arrived(unit(source, part), wz_send.at[lane, step], wz_recv.at[lane, step])
                if step < reach(direction, part):
                    send(source, direction, part, step + 1)

        def keys_of(ahead):
            head = (z_hi + ahead) % 4
            total = jnp.zeros((256, 128), F32)
            for part in range(2):
                total = total + jnp.dot(
                    tokbuf[:, pl.ds(part * HALF, HALF)],
                    wbuf[head, pl.ds(part * 4, 4)].reshape(HALF, 128),
                    preferred_element_type=F32,
                )
            kbuf[ahead] = (D ** (-0.5) * total).astype(BF).reshape(2, 2, 64, 128)
            spot = keys.at[:, pl.ds(pl.multiple_of(z_hi * 64, 64), 64), :]
            for c in range(2):
                if ahead == 0 and c == 1:
                    copy = pltpu.make_async_copy(kbuf.at[ahead, c], spot, local_sem.at[8])
                    copy.start()
                    copy.wait()
                    continue
                copy = remote(
                    kbuf.at[ahead, c], spot, key_send.at[ahead * 2 + c], key_recv.at[z_hi],
                    place(x, y, head * LO + z_lo, c),
                )
                copy.start()
                sent.append(copy)

        begun, done, near, wide = 3, 0, False, False
        line = [(0, part) for part in range(begun)]
        for _, part in line:
            own(part)
        while done < len(line):
            step, part = line[done][0] + 1, line[done][1]
            done += 1
            forward(step, part)
            if step < 6:
                line.append((step, part))
            if begun < PARTS:
                own(begun)
                line.append((0, begun))
                begun += 1
            if done == 2 * PARTS:
                outer_step()
            rest = [at for at, _ in line[done:]]
            if not near and begun == PARTS and all(at >= 2 for at in rest):
                near = True
                tokens_here()
                keys_of(0)
            if not wide and near and all(at >= 5 for at in rest):
                wide = True
                keys_of(1)
                keys_of(3)
        keys_of(2)
        for copy in sent:
            copy.wait_send()

    def make_gradient():
        sent = []
        for t in range(4):
            for c in range(2):

                @pl.when((t != z_hi) | (core != c))
                def _(t=t, c=c):
                    arrived(cotbuf.at[t, c], cot_send.at[0], cot_recv.at[t * 2 + c])

        for t in range(4):
            cotwide[:, pl.ds(t * 128, 128)] = cotbuf[t].reshape(256, 128)
        tokens_here()

        far_tile = (((y + 4) % NY) * BLOCK) // WIDE
        near_tile = (((y + 3) % NY) * BLOCK) // WIDE

        def tile(i, lead):
            columns = pl.ds(pl.multiple_of(((lead + i) % TILES) * WIDE, WIDE), WIDE)
            gbuf[columns, :] = lax.dot_general(
                tokbuf[:, columns], cotwide[...], (((0,), (0,)), ((), ())), preferred_element_type=F32
            )
            return lead

        def part_of(at_y, sub):
            rows = pl.ds(pl.multiple_of(at_y * BLOCK + sub % 2 * SHORT, 8), SHORT)
            return gbuf[rows, pl.ds(sub // 2 * 256, 256)]

        def hops(direction, sub):
            return 4 if direction == sub // 2 else 3

        def send(src, direction, sub, step, sem):
            lane = direction * 4 + sub
            copy = remote(
                src, ring.at[lane, step - 1], sem, ring_recv.at[lane, step],
                place(x, (y + (1, NY - 1)[direction]) % NY, z, 0),
            )
            copy.start()
            sent.append(copy)

        def begin(sub):
            for direction in range(2):
                far = hops(direction, sub)
                lane = direction * 4 + sub
                lead_out[lane] = part_of((y + (far, NY - far)[direction]) % NY, sub).astype(BF)
                send(lead_out.at[lane], direction, sub, 1, first_send.at[lane])

        def pass_on(step, sub):
            for direction in range(2):
                far = hops(direction, sub)
                lane = direction * 4 + sub
                if step > far:
                    continue
                arrived(ring.at[lane, step - 1], ring_send.at[lane, step], ring_recv.at[lane, step])
                if step < far:
                    left = far - step
                    block = part_of((y + (left, NY - left)[direction]) % NY, sub)
                    ring[lane, step - 1] = (ring[lane, step - 1].astype(F32) + block).astype(BF)
                    send(ring.at[lane, step - 1], direction, sub, step + 1, ring_send.at[lane, step])

        def finish(sub):
            total = part_of(y, sub)
            for direction in range(2):
                total = total + ring[direction * 4 + sub, hops(direction, sub) - 1].astype(F32)
            for k in range(2):
                zsend[sub, k] = total[:, k * 128 : k * 128 + 128].astype(BF)
                for i in range(3):
                    lo, c = divmod(sub % 2 * 3 + i, 2)
                    target_z = (sub // 2 * 2 + k) * LO + lo
                    piece = zsend.at[sub, k, pl.ds(i * ROWS, ROWS)]
                    copy = remote(
                        piece, landed.at[z], gz_send.at[(sub * 2 + k) * 3 + i], gz_recv.at[z],
                        place(x, y, target_z, c),
                    )
                    if c == 1:
                        copy.start()
                        sent.append(copy)
                        continue
                    away = target_z != z

                    @pl.when(jnp.logical_not(away))
                    def _(k=k, i=i):
                        landed[z] = zsend[sub, k, pl.ds(i * ROWS, ROWS)]

                    @pl.when(away)
                    def _(copy=copy):
                        copy.start()

                    maybe.append((away, copy))

        maybe = []
        lax.fori_loop(0, 7, tile, far_tile)
        begin(0)
        lax.fori_loop(0, 3, tile, near_tile)
        begin(2)
        lax.fori_loop(7, 11, tile, far_tile)
        begin(1)
        lax.fori_loop(11, 15, tile, far_tile)
        begin(3)
        lax.fori_loop(15, 19, tile, far_tile)
        for step in range(1, 5):
            for sub in (0, 2, 1, 3):
                pass_on(step, sub)
                if step == 4:
                    finish(sub)
            if step == 1:
                outer_step()
        for copy in sent:
            copy.wait_send()
        for when, copy in maybe:

            @pl.when(when)
            def _(copy=copy):
                copy.wait_send()

    @pl.when(in_charge)
    def _():
        make_keys()

    @pl.when(helps)
    def _():
        make_gradient()

    for from_z in range(NZ):

        @pl.when((z != from_z) | in_charge)
        def _(from_z=from_z):
            arrived(landed.at[from_z], gz_send.at[0], gz_recv.at[from_z])

    loads[3].wait()
    loads[4].wait()
    gradient = landed[0].astype(F32)
    for from_z in range(1, NZ):
        gradient = gradient + landed[from_z].astype(F32)
    gradient = D ** (-0.5) * gradient
    weights = master[...]
    one = 0.9 * first[...] + 0.1 * gradient
    two = 0.95 * second[...] + 0.05 * gradient * gradient
    one_hat = one / (1.0 - 0.9**10)
    two_hat = two / (1.0 - 0.95**10)
    adam_out[0] = weights - 0.01 * (one_hat / (jnp.sqrt(two_hat) + 1e-08) + 0.1 * weights)
    adam_out[1] = one
    adam_out[2] = two
    stores = outer_stores
    for i, dst in enumerate((new_master, new_first, new_second)):
        stores.append(pltpu.make_async_copy(adam_out.at[i], dst.at[0], local_sem.at[12 + i]))
        stores[-1].start()

    for hi in range(4):

        @pl.when((z_hi != hi) | helps)
        def _(hi=hi):
            arrived(keys.at[:, pl.ds(hi * 64, 64), :], key_send.at[0], key_recv.at[hi])

    for copy in stores:
        copy.wait()
    for when, copy in pending:
        if when is None:
            copy.wait_send()
        else:

            @pl.when(when)
            def _(copy=copy):
                copy.wait_send()


def hand_over(*refs):
    count = (len(refs) - 1) // 3
    sources, results, buffers, sems = refs[:count], refs[count : 2 * count], refs[2 * count : -1], refs[-1]
    inward = [
        pltpu.make_async_copy(src, buf, sems.at[i]) for i, (src, buf) in enumerate(zip(sources, buffers))
    ]
    outward = [
        pltpu.make_async_copy(buf, dst, sems.at[count + i])
        for i, (buf, dst) in enumerate(zip(buffers, results))
    ]
    for copy in inward:
        copy.start()
    for first, second in zip(inward, outward):
        first.wait()
        second.start()
    for copy in outward:
        copy.wait()


def on_device(
    tokens, key_cot, key_master, adam_first, adam_second, frag_local, frag_global, frag_moment, frag_order
):
    hbm = pl.BlockSpec(memory_space=pltpu.HBM)
    shape = jax.ShapeDtypeStruct
    dma = pltpu.SemaphoreType.DMA
    one = (ROWS, 128)
    two = (2, *one)
    results = (shape((2, 256, 128), BF),) + (shape((1, *one), F32),) * 3 + (shape(two, F32),) * 2 + (shape((1, *two), F32),)
    made = pl.pallas_call(
        exchange,
        out_shape=results,
        in_specs=[hbm] * 9,
        out_specs=(hbm,) * 7,
        scratch_shapes=[
            pltpu.VMEM((256, D), BF),
            pltpu.VMEM((4, 2, 2, 64, 128), BF),
            pltpu.VMEM((256, 512), BF),
            pltpu.VMEM(one, BF),
            pltpu.VMEM((4, NY, BLOCK, 128), BF),
            pltpu.VMEM((D, 512), F32),
            pltpu.VMEM((8, SHORT, 256), BF),
            pltpu.VMEM((8, 4, SHORT, 256), BF),
            pltpu.VMEM((4, 2, SHORT, 128), BF),
            pltpu.VMEM((4, 2, 2, 64, 128), BF),
            pltpu.VMEM((NZ, *one), BF),
            pltpu.VMEM((NX, *two), F32),
            pltpu.SMEM((8,), jnp.int32),
            pltpu.VMEM((8, *two), F32),
            pltpu.VMEM((8, *two), F32),
            pltpu.VMEM((8, *two), F32),
            pltpu.VMEM(one, F32),
            pltpu.VMEM(one, F32),
            pltpu.VMEM(one, F32),
            pltpu.VMEM((3, *one), F32),
            pltpu.VMEM((3, *two), F32),
            dma((15,)), dma((2,)), dma((4,)), dma((8,)), dma((NY,)), dma((2 * NY,)), dma((2 * PARTS, 7)), dma((2 * PARTS, 7)),
            dma((8,)), dma((8, 5)), dma((8, 5)), dma((24,)), dma((NZ,)), dma((8,)), dma((4,)), dma((NX,)), dma((NX,)),
        ],
        compiler_params=pltpu.CompilerParams(
            collective_id=0, has_side_effects=True, vmem_limit_bytes=60 * 1024 * 1024
        ),
    )(
        tokens.reshape(128, D), key_cot, key_master, adam_first, adam_second, frag_order, frag_local[0],
        frag_global, frag_moment,
    )
    return pl.pallas_call(
        hand_over,
        out_shape=results,
        in_specs=[hbm] * 7,
        out_specs=(hbm,) * 7,
        scratch_shapes=[pltpu.VMEM(r.shape, r.dtype) for r in results] + [dma((14,))],
        compiler_params=pltpu.CompilerParams(vmem_limit_bytes=60 * 1024 * 1024),
    )(*made)


def solution(mesh):
    return jax.shard_map(
        on_device,
        mesh=mesh,
        in_specs=(
            P(None, ("replica", "fsdp", "tensor"), None),
            P(None, ("replica", "fsdp"), "tensor"),
            P("replica", "fsdp", "tensor"),
            P("replica", "fsdp", "tensor"),
            P("replica", "fsdp", "tensor"),
            P("replica", None, None, "fsdp", "tensor"),
            P(None, None, "fsdp", "tensor"),
            P(None, None, "fsdp", "tensor"),
            P(),
        ),
        out_specs=(
            P(None, ("replica", "fsdp"), "tensor"),
            P("replica", "fsdp", "tensor"),
            P("replica", "fsdp", "tensor"),
            P("replica", "fsdp", "tensor"),
            P(None, "fsdp", "tensor"),
            P(None, "fsdp", "tensor"),
            P("replica", None, "fsdp", "tensor"),
        ),
        check_vma=False,
    )
```
